32 devices in a mesh: grp: 2 (over x), slab: 16 (over z, y, core).
Axes of the slice: x: 2, y: 2, z: 4, core: 2. Of those that a mesh axis runs over, the one named last changes fastest.
Arguments:
- states: float32 [1024, 128, 128], P(('grp', 'slab')), parts along dimension 0, may hold values from -30 to 30
- onsite_blocks: float32 [8, 128, 128], replicated, may hold values from -0.5 to 0.5
- hop_blocks: float32 [16, 128, 128], replicated, may hold values from -0.5 to 0.5
- onsite_index: int32 [1024], P(('grp', 'slab')), parts along dimension 0, may hold values from 0 to 7
- hop_index: int32 [1024, 4], P(('grp', 'slab')), parts along dimension 0, may hold values from 0 to 15, as said below
Outputs:
- basis: float32 [1024, 128, 128], P(('grp', 'slab')), parts along dimension 0
- reduced: float32 [256, 128], P('grp'), parts along dimension 0
The draws below stay inside these ranges and needn't reach their ends.
There are 2 independent parts, one for each index of `grp`. The reference program is written for one: setup_inputs(seed, part) draws one part's arguments, and reference() takes and returns one part's arrays. A program takes and returns all parts, laid end to end along the dimension named above; an argument that names none is the same for every part. Nothing has to cross between parts.
Inputs may be any that keep to these rules, and one draw needn't show every extreme that they name: Consistent coupling: for every cell c, hop_index[c+1,1] = hop_index[c,2] and hop_index[c+2,0] = hop_index[c,3].
All inputs are finite; a program needn't handle non-finite values.
Results may differ from the reference program's by a relative error of at most 0.0001.
Values sent between devices are 32-bit elements; how exact they have to be, the bound alone decides.
A program may use at most 128 MiB of HBM per device.

```python
import jax
import jax.numpy as jnp
from jax import lax

ORB = 128
NST = 128
NON = 8
NHOP = 16
DEGREE = 4
CELLS = 512


def draw_states(key, part):
    key = jax.random.fold_in(key, 11)
    first, second = jax.random.split(key, 2)
    position = jnp.arange(CELLS, dtype=jnp.float32) / max(CELLS - 1, 1)
    rough = jax.random.uniform(second, (CELLS, ORB, 1), jnp.float32, 0.5, 1.5)
    base = jnp.clip(jax.random.normal(first, (CELLS, ORB, NST), jnp.float32), -6.0, 6.0)
    scale = 3.0 ** position
    return jnp.clip(base * scale[:, None, None] * rough, -30.0, 30.0)


def draw_hop_index(key, part):
    key = jax.random.fold_in(key, 23)
    first, second = jax.random.split(key, 2)
    plus_one = jax.random.randint(first, (CELLS,), 0, NHOP).at[0].set(NHOP - 1)
    plus_two = jax.random.randint(second, (CELLS,), 0, NHOP).at[0].set(0)
    return jnp.stack([jnp.roll(plus_two, 2), jnp.roll(plus_one, 1), plus_one, plus_two], axis=1).astype(jnp.int32)


def with_ends(drawn, stream_key, low, high):
    index_at = [jax.random.randint(jax.random.fold_in(stream_key, axis), (), 0, length) for axis, length in enumerate(drawn.shape)]
    main_axis = drawn.shape.index(max(drawn.shape))
    next_to = index_at[:main_axis] + [(index_at[main_axis] + 1) % drawn.shape[main_axis]] + index_at[main_axis + 1:]
    return drawn.at[tuple(index_at)].set(low).at[tuple(next_to)].set(high)


def noise(rng, extent, spread, most, kind=jnp.bfloat16):
    entries = spread * jax.random.normal(rng, extent, jnp.float32)
    return jnp.clip(entries, min=-most, max=most).astype(kind)


def setup_inputs(seed: int = 0, part: int = 0) -> dict:
    key_list = jax.random.split(jax.random.key(seed), 6)
    part_splits = jax.random.split(jax.random.fold_in(key_list[5], part), 6)
    states = draw_states(jax.random.fold_in(jax.random.fold_in(key_list[5], part), 71), part)
    onsite_blocks = noise(key_list[1], (NON, ORB, ORB), ORB ** -0.5, 0.5, jnp.float32)
    hop_blocks = noise(key_list[2], (NHOP, ORB, ORB), ORB ** -0.5, 0.5, jnp.float32)
    onsite_index = with_ends(jax.random.randint(part_splits[3], (CELLS,), 0, NON), jax.random.fold_in(part_splits[3], 1), 0, NON - 1).astype(jnp.int32)
    hop_index = draw_hop_index(jax.random.fold_in(jax.random.fold_in(key_list[5], part), 71), part)
    return dict(states=states, onsite_blocks=onsite_blocks, hop_blocks=hop_blocks, onsite_index=onsite_index, hop_index=hop_index)


def apply_blocks(padded, onsite_sym, hop_blocks, onsite_index, hop_index):
    length = onsite_index.shape[0]
    highest = lax.Precision.HIGHEST
    result = jnp.einsum('cij,cjs->cis', onsite_sym[onsite_index], padded[2:2 + length], precision=highest)
    result = result + jnp.einsum('cij,cjs->cis', hop_blocks[hop_index[:, 2]], padded[3:3 + length], precision=highest)
    result = result + jnp.einsum('cij,cjs->cis', hop_blocks[hop_index[:, 3]], padded[4:4 + length], precision=highest)
    result = result + jnp.einsum('cji,cjs->cis', hop_blocks[hop_index[:, 1]], padded[1:1 + length], precision=highest)
    result = result + jnp.einsum('cji,cjs->cis', hop_blocks[hop_index[:, 0]], padded[0:length], precision=highest)
    return result

def reference(states, onsite_blocks, hop_blocks, onsite_index, hop_index):
    centre = 1.5
    half_width = 3.0
    highest = lax.Precision.HIGHEST
    onsite_sym = 0.5 * (onsite_blocks + jnp.swapaxes(onsite_blocks, 1, 2))

    def apply_full(field):
        padded = jnp.pad(field, ((2, 2), (0, 0), (0, 0)))
        return apply_blocks(padded, onsite_sym, hop_blocks, onsite_index, hop_index)
    previous = states
    image = apply_full(states)
    current = (image - centre * states) / half_width
    for step in range(DEGREE - 1):
        image = apply_full(current)
        following = 2.0 * (image - centre * current) / half_width - previous
        previous, current = (current, following)
    image = apply_full(current)
    gram = jnp.einsum('cis,cit->st', current, current, precision=highest)
    projected = jnp.einsum('cis,cit->st', current, image, precision=highest)
    lower = jnp.linalg.cholesky(gram)
    inverse = jax.scipy.linalg.solve_triangular(lower, jnp.eye(NST, dtype=jnp.float32), lower=True)
    reduced = jnp.dot(jnp.dot(inverse, projected, precision=highest), inverse.T, precision=highest)
    factor = jnp.sqrt(jnp.float32(CELLS * ORB))
    basis = jnp.einsum('cis,ts->cit', current, inverse, precision=highest) * factor
    return (basis, reduced)
```

```python
import functools

import jax
import jax.numpy as jnp
from jax import lax
from jax.experimental import pallas as pl
from jax.experimental.pallas import tpu as pltpu
from jax.sharding import PartitionSpec as P

DEGREE = 4
MESH = pl.DeviceIdType.MESH
BF = jnp.bfloat16
F32 = jnp.float32


def split2(x):
    hi = x.astype(BF)
    lo = (x - hi.astype(F32)).astype(BF)
    return hi, lo


def split3(x):
    hi = x.astype(BF).astype(F32)
    rest = x - hi
    mid = rest.astype(BF).astype(F32)
    return hi, mid, rest - mid


def kernel(
    n,
    owners,
    hop_idx,
    on_idx,
    states,
    onsite,
    hop,
    f4,
    inv_out,
    red_out,
    sym_t,
    half_t,
    hop_t,
    hopt_t,
    wa,
    wb,
    fa,
    fb,
    wt,
    halo_l,
    halo_r,
    gacc,
    part,
    inbox,
    share,
    full,
    aug,
    halo_send,
    halo_recv,
    rs_send,
    rs_recv,
    ag_send,
    ag_recv,
):
    me = lax.axis_index("slab")
    cells, orb, width = states.shape
    stride = n // owners
    rows = width // owners
    non = onsite.shape[0]
    nhop = hop.shape[0]

    barrier = pltpu.get_barrier_semaphore()

    @pl.loop(1, n)
    def _(d):
        pl.semaphore_signal(
            barrier, inc=1, device_id={"slab": lax.rem(me + d, n)}, device_id_type=MESH
        )

    def put(w, at, x):
        hi, lo = split2(x)
        w[at, :, 0:width] = hi
        w[at, :, width : 2 * width] = lo

    def table(ref, at, x):
        hi, lo = split2(x)
        ref[at, 0:orb, :] = hi
        ref[at, orb : 2 * orb, :] = lo

    zero2 = jnp.zeros((2, orb, 2 * width), BF)
    for w in (wa, wb):
        w[0:2] = zero2
        w[cells + 2 : cells + 4] = zero2

    pl.semaphore_wait(barrier, n - 1)

    def halo(k, src):
        left = pltpu.make_async_remote_copy(
            src_ref=src.at[0:2],
            dst_ref=halo_r.at[k],
            send_sem=halo_send.at[k, 0],
            recv_sem=halo_recv.at[k, 0],
            device_id={"slab": jnp.maximum(me - 1, 0)},
            device_id_type=MESH,
        )
        right = pltpu.make_async_remote_copy(
            src_ref=src.at[cells - 2 : cells],
            dst_ref=halo_l.at[k],
            send_sem=halo_send.at[k, 1],
            recv_sem=halo_recv.at[k, 1],
            device_id={"slab": jnp.minimum(me + 1, n - 1)},
            device_id_type=MESH,
        )
        return left, right

    def halo_start(k, src):
        left, right = halo(k, src)
        pl.when(me > 0)(left.start)
        if k < DEGREE:
            pl.when(me < n - 1)(right.start)

    def halo_wait(k, src, w):
        left, right = halo(k, src)

        @pl.when(me > 0)
        def _():
            left.wait_send()
            if k < DEGREE:
                right.wait_recv()
                for i in range(2):
                    put(w, i, halo_l[k, i])

        @pl.when(me < n - 1)
        def _():
            if k < DEGREE:
                right.wait_send()
            left.wait_recv()
            for i in range(2):
                put(w, cells + 2 + i, halo_r[k, i])

    halo_start(0, states)

    @pl.loop(0, non)
    def _(i):
        block = onsite[i]
        sym = 0.5 * (block + block.T)
        table(sym_t, i, sym)
        table(half_t, i, 0.5 * sym)

    @pl.loop(0, nhop)
    def _(i):
        block = hop[i]
        table(hop_t, i, block)
        table(hopt_t, i, block.T)

    @pl.loop(0, cells)
    def _(c):
        put(wa, c + 2, states[c])

    halo_wait(0, states, wa)

    def fold(acc):
        return acc[:orb, :width] + (acc[:orb, width:] + acc[orb:, :width])

    def apply_cell(w, c):
        lhs = jnp.concatenate(
            [
                hopt_t[hop_idx[c, 0]],
                hopt_t[hop_idx[c, 1]],
                sym_t[on_idx[c]],
                hop_t[hop_idx[c, 2]],
                hop_t[hop_idx[c, 3]],
            ],
            axis=1,
        )
        rhs = w[pl.ds(c, 5)].reshape(5 * orb, 2 * width)
        return fold(jnp.dot(lhs, rhs, preferred_element_type=F32))

    def step(k, w, w_next, cur, prev, out):
        def one(c):
            image = apply_cell(w, c)
            if k == 0:
                new = (image - 1.5 * cur[c]) * (1.0 / 3.0)
            else:
                new = (image - 1.5 * cur[c]) * (2.0 / 3.0) - prev[c]
            out[c] = new
            put(w_next, c + 2, new)
            if k == DEGREE - 1:
                hi, lo = split2(new.T)
                wt[c, 0:width, :] = hi
                wt[c, width : 2 * width, :] = lo

        for c in (0, 1, cells - 2, cells - 1):
            one(c)
        halo_start(k + 1, out)

        @pl.loop(2, cells - 2, step=4)
        def _(c):
            for i in range(4):
                one(c + i)

    step(0, wa, wb, states, None, fa)
    halo_wait(1, fa, wb)
    step(1, wb, wa, fa, states, fb)
    halo_wait(2, fb, wa)
    step(2, wa, wb, fb, fa, fa)
    halo_wait(3, fa, wb)
    step(3, wb, wa, fa, fb, f4)

    def rs_copy(s, t):
        return pltpu.make_async_remote_copy(
            src_ref=part.at[s, pl.ds(t * rows, rows)],
            dst_ref=inbox.at[s, me],
            send_sem=rs_send.at[s, t],
            recv_sem=rs_recv.at[s, me],
            device_id={"slab": t * stride},
            device_id_type=MESH,
        )

    def rs_start(s):
        @pl.loop(0, owners)
        def _(t):
            @pl.when(t * stride != me)
            def _():
                rs_copy(s, t).start()

    mine = me // stride

    def ag_copy(s, d):
        return pltpu.make_async_remote_copy(
            src_ref=share.at[s],
            dst_ref=full.at[s, pl.ds(mine * rows, rows)],
            send_sem=ag_send.at[s, d],
            recv_sem=ag_recv.at[s, mine],
            device_id={"slab": lax.rem(me + d, n)},
            device_id_type=MESH,
        )

    def owner(f):
        if stride == 1:
            f()
        else:
            pl.when(me == mine * stride)(f)

    def rs_finish(s):
        @pl.loop(0, owners)
        def _(t):
            @pl.when(t * stride != me)
            def _():
                rs_copy(s, t).wait_send()

        @owner
        def _():
            share[s] = part[s, pl.ds(mine * rows, rows)]

            @pl.loop(1, n)
            def _(d):
                src = lax.rem(me + d, n)
                pltpu.make_async_remote_copy(
                    src_ref=inbox.at[s, src],
                    dst_ref=inbox.at[s, src],
                    send_sem=rs_send.at[s, 0],
                    recv_sem=rs_recv.at[s, src],
                    device_id={"slab": src},
                    device_id_type=MESH,
                ).wait_recv()
                share[s] = share[s] + inbox[s, src]

            @pl.loop(1, n)
            def _(d):
                ag_copy(s, d).start()

            full[s, pl.ds(mine * rows, rows)] = share[s]

    def ag_finish(s):
        @owner
        def _():
            @pl.loop(1, n)
            def _(d):
                ag_copy(s, d).wait_send()

        @pl.loop(0, owners)
        def _(t):
            @pl.when(t * stride != me)
            def _():
                pltpu.make_async_remote_copy(
                    src_ref=share.at[s],
                    dst_ref=full.at[s, pl.ds(t * rows, rows)],
                    send_sem=ag_send.at[s, 0],
                    recv_sem=ag_recv.at[s, t],
                    device_id={"slab": t * stride},
                    device_id_type=MESH,
                ).wait_recv()

    gacc[...] = jnp.zeros_like(gacc)

    @pl.loop(0, cells, step=4)
    def _(c):
        lhs = jnp.concatenate([wt[c + i] for i in range(4)], axis=1)
        rhs = wa[pl.ds(c + 2, 4)].reshape(4 * orb, 2 * width)
        gacc[...] += jnp.dot(lhs, rhs, preferred_element_type=F32)

    part[0] = fold(gacc)
    rs_start(0)

    gacc[...] = jnp.zeros_like(gacc)

    def half_image(c):
        lhs = jnp.concatenate(
            [half_t[on_idx[c]], hop_t[hop_idx[c, 2]], hop_t[hop_idx[c, 3]]], axis=1
        )
        rhs = wa[pl.ds(c + 2, 3)].reshape(3 * orb, 2 * width)
        return fold(jnp.dot(lhs, rhs, preferred_element_type=F32))

    def project(c):
        images = []
        for i in range(4):
            hi, lo = split2(half_image(c + i))
            images.append(jnp.concatenate([hi, lo], axis=1))
        lhs = jnp.concatenate([wt[c + i] for i in range(4)], axis=1)
        gacc[...] += jnp.dot(
            lhs, jnp.concatenate(images, axis=0), preferred_element_type=F32
        )

    middle = cells // 2

    @pl.loop(0, middle, step=4)
    def _(c):
        project(c)

    rs_finish(0)
    halo_wait(4, f4, wa)

    @pl.loop(middle, cells, step=4)
    def _(c):
        project(c)

    part[1] = fold(gacc)
    rs_start(1)

    ag_finish(0)
    aug[:, 0:width] = full[0]
    row = lax.broadcasted_iota(jnp.int32, (width, width), 0)
    col = lax.broadcasted_iota(jnp.int32, (width, width), 1)
    aug[:, width : 2 * width] = jnp.where(row == col, 1.0, 0.0).astype(F32)

    def chol_block(b):
        base = 8 * b
        panel = aug[base : base + 8, :]
        s = {}
        for i in range(8):
            for k in range(i, 8):
                s[i, k] = jnp.broadcast_to(
                    panel[i : i + 1, base + k : base + k + 1], (1, 2 * width)
                )
        lines = [panel[i : i + 1, :] for i in range(8)]
        done = []
        for i in range(8):
            inv = lax.rsqrt(s[i, i])
            line = lines[i] * inv
            done.append(line)
            low = {k: s[i, k] * inv for k in range(i + 1, 8)}
            for k in range(i + 1, 8):
                lines[k] = lines[k] - low[k] * line
                for m in range(k, 8):
                    s[k, m] = s[k, m] - low[k] * low[m]
        upper = jnp.concatenate(done, axis=0)
        aug[base : base + 8, :] = upper
        if base + 8 < width:
            hi, mid, lo = split3(upper)
            left = jnp.concatenate([hi, hi, mid, hi, mid, lo], axis=0)[:, 0:width]
            right = jnp.concatenate([hi, mid, hi, lo, mid, hi], axis=0)
            update = lax.dot_general(
                left.T.astype(BF),
                right.astype(BF),
                (((1,), (0,)), ((), ())),
                preferred_element_type=F32,
            )
            aug[base + 8 :, :] = aug[base + 8 :, :] - update[base + 8 :, :]

    blocks = width // 8
    for b in range(blocks // 2):
        chol_block(b)
    rs_finish(1)
    for b in range(blocks // 2, blocks):
        chol_block(b)
    ag_finish(1)

    inverse = aug[:, width : 2 * width]
    inv_out[...] = inverse
    upper = full[1]
    projected = upper + upper.T
    highest = lax.Precision.HIGHEST
    right = jnp.dot(inverse, projected, precision=highest, preferred_element_type=F32)
    red_out[...] = lax.dot_general(
        right,
        inverse,
        (((1,), (1,)), ((), ())),
        precision=highest,
        preferred_element_type=F32,
    )


def local(states, onsite_blocks, hop_blocks, onsite_index, hop_index):
    cells, orb, width = states.shape
    n = lax.axis_size("slab")
    owners = min(n, width // 8)
    rows = width // owners
    non, nhop = onsite_blocks.shape[0], hop_blocks.shape[0]
    vmem = pl.BlockSpec(memory_space=pltpu.VMEM)
    smem = pl.BlockSpec(memory_space=pltpu.SMEM)
    field = pltpu.VMEM((cells, orb, width), F32)
    wide = pltpu.VMEM((cells + 4, orb, 2 * width), BF)
    halo = pltpu.VMEM((DEGREE + 1, 2, orb, width), F32)
    dma = pltpu.SemaphoreType.DMA
    current, inverse, reduced = pl.pallas_call(
        functools.partial(kernel, n, owners),
        out_shape=(
            jax.ShapeDtypeStruct((cells, orb, width), F32),
            jax.ShapeDtypeStruct((width, width), F32),
            jax.ShapeDtypeStruct((width, width), F32),
        ),
        in_specs=[smem, smem, vmem, vmem, vmem],
        out_specs=(vmem, vmem, vmem),
        scratch_shapes=[
            pltpu.VMEM((non, 2 * orb, orb), BF),
            pltpu.VMEM((non, 2 * orb, orb), BF),
            pltpu.VMEM((nhop, 2 * orb, orb), BF),
            pltpu.VMEM((nhop, 2 * orb, orb), BF),
            wide,
            wide,
            field,
            field,
            pltpu.VMEM((cells, 2 * width, orb), BF),
            halo,
            halo,
            pltpu.VMEM((2 * width, 2 * width), F32),
            pltpu.VMEM((2, width, width), F32),
            pltpu.VMEM((2, n, rows, width), F32),
            pltpu.VMEM((2, rows, width), F32),
            pltpu.VMEM((2, width, width), F32),
            pltpu.VMEM((width, 2 * width), F32),
            dma((DEGREE + 1, 2)),
            dma((DEGREE + 1, 2)),
            dma((2, owners)),
            dma((2, n)),
            dma((2, n)),
            dma((2, owners)),
        ],
        compiler_params=pltpu.CompilerParams(
            collective_id=0, has_side_effects=True, vmem_limit_bytes=50 * 2**20
        ),
        name="filter",
    )(hop_index, onsite_index, states, onsite_blocks, hop_blocks)
    total = cells * n
    factor = jnp.sqrt(jnp.float32(total * orb))
    basis = jnp.einsum(
        "cis,ts->cit", current, inverse * factor, precision=lax.Precision.HIGH
    )
    return (basis, reduced)


def solution(mesh):
    placed = (
        P(("grp", "slab"), None, None),
        P(),
        P(),
        P(("grp", "slab")),
        P(("grp", "slab"), None),
    )
    return jax.shard_map(
        local,
        mesh=mesh,
        in_specs=placed,
        out_specs=(P(("grp", "slab"), None, None), P("grp", None)),
        check_vma=False,
    )
```

```python
import functools

import jax
import jax.numpy as jnp
from jax import lax
from jax.experimental import pallas as pl
from jax.experimental.pallas import tpu as pltpu
from jax.sharding import PartitionSpec as P

DEGREE = 4
MESH = pl.DeviceIdType.MESH
BF = jnp.bfloat16
F32 = jnp.float32


def split2(x):
    hi = x.astype(BF)
    lo = (x - hi.astype(F32)).astype(BF)
    return hi, lo


def split3(x):
    hi = x.astype(BF).astype(F32)
    rest = x - hi
    mid = rest.astype(BF).astype(F32)
    return hi, mid, rest - mid


def kernel(
    n,
    owners,
    hop_idx,
    on_idx,
    states_hbm,
    onsite_hbm,
    hop_hbm,
    wide_out,
    inv_out,
    proj_out,
    states,
    onsite,
    hop,
    sym_t,
    half_t,
    hop_t,
    hopt_t,
    wa,
    wb,
    fa,
    fb,
    wt,
    halo_l,
    halo_r,
    gacc,
    part,
    inbox,
    share,
    full,
    aug,
    halo_send,
    halo_recv,
    rs_send,
    rs_recv,
    ag_send,
    ag_recv,
    load_sem,
    store_sem,
):
    me = lax.axis_index("slab")
    cells, orb, width = states.shape
    stride = n // owners
    rows = width // owners
    non = onsite.shape[0]
    nhop = hop.shape[0]

    barrier = pltpu.get_barrier_semaphore()

    @pl.loop(1, n)
    def _(d):
        pl.semaphore_signal(
            barrier, inc=1, device_id={"slab": lax.rem(me + d, n)}, device_id_type=MESH
        )

    loads = [
        pltpu.make_async_copy(src, dst, load_sem.at[i])
        for i, (src, dst) in enumerate(
            ((hop_hbm, hop), (onsite_hbm, onsite), (states_hbm, states))
        )
    ]
    for load in loads:
        load.start()

    def put(w, at, x):
        hi, lo = split2(x)
        w[at, :, 0:width] = hi
        w[at, :, width : 2 * width] = lo

    def table(ref, at, x):
        hi, lo = split2(x)
        ref[at, :, 0:orb] = hi
        ref[at, :, orb : 2 * orb] = lo

    zero2 = jnp.zeros((2, orb, 2 * width), BF)
    for w in (wa, wb):
        w[0:2] = zero2
        w[cells + 2 : cells + 4] = zero2

    pl.semaphore_wait(barrier, n - 1)

    def halo(k, src):
        left = pltpu.make_async_remote_copy(
            src_ref=src.at[0:2],
            dst_ref=halo_r.at[k],
            send_sem=halo_send.at[k, 0],
            recv_sem=halo_recv.at[k, 0],
            device_id={"slab": jnp.maximum(me - 1, 0)},
            device_id_type=MESH,
        )
        right = pltpu.make_async_remote_copy(
            src_ref=src.at[cells - 2 : cells],
            dst_ref=halo_l.at[k],
            send_sem=halo_send.at[k, 1],
            recv_sem=halo_recv.at[k, 1],
            device_id={"slab": jnp.minimum(me + 1, n - 1)},
            device_id_type=MESH,
        )
        return left, right

    def halo_start(k, src):
        left, right = halo(k, src)
        pl.when(me > 0)(left.start)
        if k < DEGREE:
            pl.when(me < n - 1)(right.start)

    def halo_wait(k, src, w):
        left, right = halo(k, src)

        @pl.when(me > 0)
        def _():
            left.wait_send()
            if k < DEGREE:
                right.wait_recv()
                for i in range(2):
                    put(w, i, halo_l[k, i])

        @pl.when(me < n - 1)
        def _():
            if k < DEGREE:
                right.wait_send()
            left.wait_recv()
            for i in range(2):
                put(w, cells + 2 + i, halo_r[k, i])

    halo_start(0, states_hbm)

    loads[0].wait()
    loads[1].wait()

    @pl.loop(0, non, unroll=True)
    def _(i):
        block = onsite[i]
        sym = 0.5 * (block + block.T)
        table(sym_t, i, sym)
        table(half_t, i, 0.5 * sym)

    @pl.loop(0, nhop, unroll=4)
    def _(i):
        block = hop[i]
        table(hop_t, i, block)
        table(hopt_t, i, block.T)

    loads[2].wait()

    @pl.loop(0, cells, unroll=4)
    def _(c):
        put(wa, c + 2, states[c])

    halo_wait(0, states_hbm, wa)

    def fold(acc):
        return acc[:, :width] + acc[:, width:]

    def twice(w, at, count):
        parts = []
        for i in range(count):
            block = w[at + i]
            parts += [block, block]
        return jnp.concatenate(parts, axis=0)

    def apply_cell(w, c):
        lhs = jnp.concatenate(
            [
                hopt_t[hop_idx[0, c]],
                hopt_t[hop_idx[1, c]],
                sym_t[on_idx[c]],
                hop_t[hop_idx[2, c]],
                hop_t[hop_idx[3, c]],
            ],
            axis=1,
        )
        return fold(jnp.dot(lhs, twice(w, c, 5), preferred_element_type=F32))

    def step(k, w, w_next, cur, prev, out):
        def one(c):
            image = apply_cell(w, c)
            if k == 0:
                new = (image - 1.5 * cur[c]) * (1.0 / 3.0)
            else:
                new = (image - 1.5 * cur[c]) * (2.0 / 3.0) - prev[c]
            out[c] = new
            put(w_next, c + 2, new)
            if k == DEGREE - 1:
                hi, lo = split2(new.T)
                wt[c, :, 0:orb] = hi
                wt[c, :, orb : 2 * orb] = lo

        for c in (0, 1, cells - 2, cells - 1):
            one(c)
        halo_start(k + 1, out)

        inner = cells - 4
        group = max(d for d in range(1, 15) if inner % d == 0)

        @pl.loop(2, cells - 2, step=group)
        def _(c):
            for i in range(group):
                one(c + i)

    step(0, wa, wb, states, None, fa)
    halo_wait(1, fa, wb)
    step(1, wb, wa, fa, states, fb)
    halo_wait(2, fb, wa)
    step(2, wa, wb, fb, fa, fa)
    halo_wait(3, fa, wb)
    step(3, wb, wa, fa, fb, fb)
    store = pltpu.make_async_copy(
        wa.at[2 : cells + 2], wide_out, store_sem
    )
    store.start()

    def rs_copy(s, t):
        return pltpu.make_async_remote_copy(
            src_ref=part.at[s, pl.ds(t * rows, rows)],
            dst_ref=inbox.at[s, me],
            send_sem=rs_send.at[s, t],
            recv_sem=rs_recv.at[s, me],
            device_id={"slab": t * stride},
            device_id_type=MESH,
        )

    def rs_start(s):
        @pl.loop(0, owners)
        def _(t):
            @pl.when(t * stride != me)
            def _():
                rs_copy(s, t).start()

    mine = me // stride

    def ag_copy(s, d):
        return pltpu.make_async_remote_copy(
            src_ref=share.at[s],
            dst_ref=full.at[s, pl.ds(mine * rows, rows)],
            send_sem=ag_send.at[s, d],
            recv_sem=ag_recv.at[s, mine],
            device_id={"slab": lax.rem(me + d, n)},
            device_id_type=MESH,
        )

    def owner(f):
        if stride == 1:
            f()
        else:
            pl.when(me == mine * stride)(f)

    def rs_finish(s):
        @pl.loop(0, owners)
        def _(t):
            @pl.when(t * stride != me)
            def _():
                rs_copy(s, t).wait_send()

        @owner
        def _():
            share[s] = part[s, pl.ds(mine * rows, rows)]

            @pl.loop(1, n)
            def _(d):
                src = lax.rem(me + d, n)
                pltpu.make_async_remote_copy(
                    src_ref=inbox.at[s, src],
                    dst_ref=inbox.at[s, src],
                    send_sem=rs_send.at[s, 0],
                    recv_sem=rs_recv.at[s, src],
                    device_id={"slab": src},
                    device_id_type=MESH,
                ).wait_recv()
                share[s] = share[s] + inbox[s, src]

            @pl.loop(1, n)
            def _(d):
                ag_copy(s, d).start()

            full[s, pl.ds(mine * rows, rows)] = share[s]

    def ag_finish(s):
        @owner
        def _():
            @pl.loop(1, n)
            def _(d):
                ag_copy(s, d).wait_send()

        @pl.loop(0, owners)
        def _(t):
            @pl.when(t * stride != me)
            def _():
                pltpu.make_async_remote_copy(
                    src_ref=share.at[s],
                    dst_ref=full.at[s, pl.ds(t * rows, rows)],
                    send_sem=ag_send.at[s, 0],
                    recv_sem=ag_recv.at[s, t],
                    device_id={"slab": t * stride},
                    device_id_type=MESH,
                ).wait_recv()

    batch = max(d for d in range(1, 9) if cells % (2 * d) == 0)
    gacc[...] = jnp.zeros_like(gacc)

    @pl.loop(0, cells, step=batch)
    def _(c):
        lhs = jnp.concatenate([wt[c + i] for i in range(batch)], axis=1)
        gacc[...] += jnp.dot(
            lhs, twice(wa, c + 2, batch), preferred_element_type=F32
        )

    part[0] = fold(gacc)
    rs_start(0)

    gacc[...] = jnp.zeros_like(gacc)

    def half_image(c):
        lhs = jnp.concatenate(
            [half_t[on_idx[c]], hop_t[hop_idx[2, c]], hop_t[hop_idx[3, c]]], axis=1
        )
        return fold(jnp.dot(lhs, twice(wa, c + 2, 3), preferred_element_type=F32))

    def project(c):
        images = []
        for i in range(batch):
            hi, lo = split2(half_image(c + i))
            both = jnp.concatenate([hi, lo], axis=1)
            images += [both, both]
        lhs = jnp.concatenate([wt[c + i] for i in range(batch)], axis=1)
        gacc[...] += jnp.dot(
            lhs, jnp.concatenate(images, axis=0), preferred_element_type=F32
        )

    middle = cells // 2

    @pl.loop(0, middle, step=batch)
    def _(c):
        project(c)

    rs_finish(0)
    halo_wait(4, fb, wa)

    @pl.loop(middle, cells, step=batch)
    def _(c):
        project(c)

    part[1] = fold(gacc)
    rs_start(1)

    ag_finish(0)
    aug[:, 0:width] = full[0]
    row = lax.broadcasted_iota(jnp.int32, (width, width), 0)
    col = lax.broadcasted_iota(jnp.int32, (width, width), 1)
    aug[:, width : 2 * width] = jnp.where(row == col, 1.0, 0.0).astype(F32)

    def chol_block(b):
        base = 8 * b
        panel = aug[base : base + 8, :]
        s = {}
        for i in range(8):
            for k in range(i, 8):
                s[i, k] = jnp.broadcast_to(
                    panel[i : i + 1, base + k : base + k + 1], (1, 2 * width)
                )
        lines = [panel[i : i + 1, :] for i in range(8)]
        done = []
        for i in range(8):
            inv = lax.rsqrt(s[i, i])
            line = lines[i] * inv
            done.append(line)
            low = {k: s[i, k] * inv for k in range(i + 1, 8)}
            for k in range(i + 1, 8):
                lines[k] = lines[k] - low[k] * line
                for m in range(k, 8):
                    s[k, m] = s[k, m] - low[k] * low[m]
        upper = jnp.concatenate(done, axis=0)
        aug[base : base + 8, :] = upper
        if base + 8 < width:
            hi, mid, lo = split3(upper)
            left = jnp.concatenate([hi, hi, mid, hi, mid, lo], axis=0)[:, 0:width]
            right = jnp.concatenate([hi, mid, hi, lo, mid, hi], axis=0)
            update = lax.dot_general(
                left.T.astype(BF),
                right.astype(BF),
                (((1,), (0,)), ((), ())),
                preferred_element_type=F32,
            )
            aug[base + 8 :, :] = aug[base + 8 :, :] - update[base + 8 :, :]

    blocks = width // 8
    for b in range(blocks // 2):
        chol_block(b)
    rs_finish(1)
    for b in range(blocks // 2, blocks):
        chol_block(b)
    ag_finish(1)

    inv_out[...] = aug[:, width : 2 * width]
    upper = full[1]
    proj_out[...] = upper + upper.T
    store.wait()


def finish(factor, wide, inv, proj, basis, reduced, weights):
    count, orb, double = wide.shape
    width = double // 2
    inverse = inv[...]

    @pl.when(pl.program_id(0) == 0)
    def _():
        hi, lo = split2(inverse.T * factor)
        for i in range(2):
            weights[i * width : (i + 1) * width, 0:width] = hi
            weights[i * width : (i + 1) * width, width : 2 * width] = lo

    both = jnp.dot(
        wide[...].reshape(count * orb, double),
        weights[...],
        preferred_element_type=F32,
    )
    basis[...] = (both[:, :width] + both[:, width:]).reshape(count, orb, width)

    @pl.when(pl.program_id(0) == 0)
    def _():
        highest = lax.Precision.HIGHEST
        right = jnp.dot(
            inverse, proj[...], precision=highest, preferred_element_type=F32
        )
        reduced[...] = lax.dot_general(
            right,
            inverse,
            (((1,), (1,)), ((), ())),
            precision=highest,
            preferred_element_type=F32,
        )


def local(states, onsite_blocks, hop_blocks, onsite_index, hop_index):
    cells, orb, width = states.shape
    n = lax.axis_size("slab")
    owners = min(n, width // 8)
    rows = width // owners
    non, nhop = onsite_blocks.shape[0], hop_blocks.shape[0]
    vmem = pl.BlockSpec(memory_space=pltpu.VMEM)
    hbm = pl.BlockSpec(memory_space=pl.ANY)
    smem = pl.BlockSpec(memory_space=pltpu.SMEM)
    field = pltpu.VMEM((cells, orb, width), F32)
    wide = pltpu.VMEM((cells + 4, orb, 2 * width), BF)
    halo = pltpu.VMEM((DEGREE + 1, 2, orb, width), F32)
    dma = pltpu.SemaphoreType.DMA
    current, inverse, projected = pl.pallas_call(
        functools.partial(kernel, n, owners),
        out_shape=(
            jax.ShapeDtypeStruct((cells, orb, 2 * width), BF),
            jax.ShapeDtypeStruct((width, width), F32),
            jax.ShapeDtypeStruct((width, width), F32),
        ),
        in_specs=[smem, smem, hbm, hbm, hbm],
        out_specs=(hbm, vmem, vmem),
        scratch_shapes=[
            field,
            pltpu.VMEM((non, orb, orb), F32),
            pltpu.VMEM((nhop, orb, orb), F32),
            pltpu.VMEM((non, orb, 2 * orb), BF),
            pltpu.VMEM((non, orb, 2 * orb), BF),
            pltpu.VMEM((nhop, orb, 2 * orb), BF),
            pltpu.VMEM((nhop, orb, 2 * orb), BF),
            wide,
            wide,
            field,
            field,
            pltpu.VMEM((cells, width, 2 * orb), BF),
            halo,
            halo,
            pltpu.VMEM((width, 2 * width), F32),
            pltpu.VMEM((2, width, width), F32),
            pltpu.VMEM((2, n, rows, width), F32),
            pltpu.VMEM((2, rows, width), F32),
            pltpu.VMEM((2, width, width), F32),
            pltpu.VMEM((width, 2 * width), F32),
            dma((DEGREE + 1, 2)),
            dma((DEGREE + 1, 2)),
            dma((2, owners)),
            dma((2, n)),
            dma((2, n)),
            dma((2, owners)),
            dma((3,)),
            dma,
        ],
        compiler_params=pltpu.CompilerParams(
            collective_id=0, has_side_effects=True, vmem_limit_bytes=60 * 2**20
        ),
        name="filter",
    )(hop_index.T, onsite_index, states, onsite_blocks, hop_blocks)
    total = cells * n
    factor = float(total * orb) ** 0.5
    count = max(d for d in range(1, 9) if cells % d == 0)
    square = pl.BlockSpec((width, width), lambda i: (0, 0))
    basis, reduced = pl.pallas_call(
        functools.partial(finish, factor),
        grid=(cells // count,),
        out_shape=(
            jax.ShapeDtypeStruct((cells, orb, width), F32),
            jax.ShapeDtypeStruct((width, width), F32),
        ),
        in_specs=[
            pl.BlockSpec((count, orb, 2 * width), lambda i: (i, 0, 0)),
            square,
            square,
        ],
        out_specs=(pl.BlockSpec((count, orb, width), lambda i: (i, 0, 0)), square),
        scratch_shapes=[pltpu.VMEM((2 * width, 2 * width), BF)],
        compiler_params=pltpu.CompilerParams(vmem_limit_bytes=32 * 2**20),
        name="finish",
    )(current, inverse, projected)
    return (basis, reduced)


def solution(mesh):
    placed = (
        P(("grp", "slab"), None, None),
        P(),
        P(),
        P(("grp", "slab")),
        P(("grp", "slab"), None),
    )
    return jax.shard_map(
        local,
        mesh=mesh,
        in_specs=placed,
        out_specs=(P(("grp", "slab"), None, None), P("grp", None)),
        check_vma=False,
    )
```

```python
import functools

import jax
import jax.numpy as jnp
from jax import lax
from jax.experimental import pallas as pl
from jax.experimental.pallas import tpu as pltpu
from jax.sharding import PartitionSpec as P

DEGREE = 4
MESH = pl.DeviceIdType.MESH
BF = jnp.bfloat16
F32 = jnp.float32


def split2(x):
    hi = x.astype(BF)
    lo = (x - hi.astype(F32)).astype(BF)
    return hi, lo


def dot_halves(a, b):
    b_both = jnp.concatenate(split2(b), axis=1)
    both = jnp.dot(
        jnp.concatenate(split2(a), axis=1),
        jnp.concatenate([b_both, b_both], axis=0),
        preferred_element_type=F32,
    )
    half = b.shape[1]
    return both[:, :half] + both[:, half:]


def split3(x):
    hi = x.astype(BF).astype(F32)
    rest = x - hi
    mid = rest.astype(BF).astype(F32)
    return hi, mid, rest - mid


def kernel(
    n,
    owners,
    hop_idx,
    on_idx,
    states_hbm,
    onsite_hbm,
    hop_hbm,
    wide_out,
    inv_out,
    proj_out,
    states,
    onsite,
    hop,
    sym_t,
    half_t,
    hop_t,
    hopt_t,
    wa,
    wb,
    fa,
    fb,
    wt,
    halo_l,
    halo_r,
    gacc,
    part,
    inbox,
    share,
    full,
    aug,
    halo_send,
    halo_recv,
    rs_send,
    rs_recv,
    ag_send,
    ag_recv,
    load_sem,
    store_sem,
):
    me = lax.axis_index("slab")
    cells, orb, width = states.shape
    stride = n // owners
    rows = width // owners
    non = onsite.shape[0]
    nhop = hop.shape[0]

    barrier = pltpu.get_barrier_semaphore()

    @pl.loop(1, n)
    def _(d):
        pl.semaphore_signal(
            barrier, inc=1, device_id={"slab": lax.rem(me + d, n)}, device_id_type=MESH
        )

    loads = [
        pltpu.make_async_copy(src, dst, load_sem.at[i])
        for i, (src, dst) in enumerate(
            ((hop_hbm, hop), (onsite_hbm, onsite), (states_hbm, states))
        )
    ]
    for load in loads:
        load.start()

    def put(w, at, x):
        hi, lo = split2(x)
        w[at, :, 0:width] = hi
        w[at, :, width : 2 * width] = lo

    def table(ref, at, x):
        hi, lo = split2(x)
        ref[at, :, 0:orb] = hi
        ref[at, :, orb : 2 * orb] = lo

    zero2 = jnp.zeros((2, orb, 2 * width), BF)
    for w in (wa, wb):
        w[0:2] = zero2
        w[cells + 2 : cells + 4] = zero2

    pl.semaphore_wait(barrier, n - 1)

    def halo(k, src):
        left = pltpu.make_async_remote_copy(
            src_ref=src.at[0:2],
            dst_ref=halo_r.at[k],
            send_sem=halo_send.at[k, 0],
            recv_sem=halo_recv.at[k, 0],
            device_id={"slab": jnp.maximum(me - 1, 0)},
            device_id_type=MESH,
        )
        right = pltpu.make_async_remote_copy(
            src_ref=src.at[cells - 2 : cells],
            dst_ref=halo_l.at[k],
            send_sem=halo_send.at[k, 1],
            recv_sem=halo_recv.at[k, 1],
            device_id={"slab": jnp.minimum(me + 1, n - 1)},
            device_id_type=MESH,
        )
        return left, right

    def halo_start(k, src):
        left, right = halo(k, src)
        pl.when(me > 0)(left.start)
        if k < DEGREE:
            pl.when(me < n - 1)(right.start)

    def halo_wait(k, src, w):
        left, right = halo(k, src)

        @pl.when(me > 0)
        def _():
            left.wait_send()
            if k < DEGREE:
                right.wait_recv()
                for i in range(2):
                    put(w, i, halo_l[k, i])

        @pl.when(me < n - 1)
        def _():
            if k < DEGREE:
                right.wait_send()
            left.wait_recv()
            for i in range(2):
                put(w, cells + 2 + i, halo_r[k, i])

    halo_start(0, states_hbm)

    loads[0].wait()
    loads[1].wait()

    @pl.loop(0, non, unroll=True)
    def _(i):
        block = onsite[i]
        sym = 0.5 * (block + block.T)
        table(sym_t, i, sym)
        table(half_t, i, 0.5 * sym)

    @pl.loop(0, nhop, unroll=4)
    def _(i):
        block = hop[i]
        table(hop_t, i, block)
        table(hopt_t, i, block.T)

    loads[2].wait()

    @pl.loop(0, cells, unroll=4)
    def _(c):
        put(wa, c + 2, states[c])

    halo_wait(0, states_hbm, wa)

    def fold(acc):
        return acc[:, :width] + acc[:, width:]

    def twice(w, at, count):
        parts = []
        for i in range(count):
            block = w[at + i]
            parts += [block, block]
        return jnp.concatenate(parts, axis=0)

    def apply_cell(w, c):
        lhs = jnp.concatenate(
            [
                hopt_t[hop_idx[0, c]],
                hopt_t[hop_idx[1, c]],
                sym_t[on_idx[c]],
                hop_t[hop_idx[2, c]],
                hop_t[hop_idx[3, c]],
            ],
            axis=1,
        )
        return fold(jnp.dot(lhs, twice(w, c, 5), preferred_element_type=F32))

    def step(k, w, w_next, cur, prev, out):
        def one(c):
            image = apply_cell(w, c)
            if k == 0:
                new = (image - 1.5 * cur[c]) * (1.0 / 3.0)
            else:
                new = (image - 1.5 * cur[c]) * (2.0 / 3.0) - prev[c]
            out[c] = new
            put(w_next, c + 2, new)
            if k == DEGREE - 1:
                hi, lo = split2(new.T)
                wt[c, :, 0:orb] = hi
                wt[c, :, orb : 2 * orb] = lo

        for c in (0, 1, cells - 2, cells - 1):
            one(c)
        halo_start(k + 1, out)

        inner = cells - 4
        group = max(d for d in range(1, 15) if inner % d == 0)

        @pl.loop(2, cells - 2, step=group)
        def _(c):
            for i in range(group):
                one(c + i)

    step(0, wa, wb, states, None, fa)
    halo_wait(1, fa, wb)
    step(1, wb, wa, fa, states, fb)
    halo_wait(2, fb, wa)
    step(2, wa, wb, fb, fa, fa)
    halo_wait(3, fa, wb)
    step(3, wb, wa, fa, fb, fb)
    store = pltpu.make_async_copy(
        wa.at[2 : cells + 2], wide_out, store_sem
    )
    store.start()

    def rs_copy(s, t):
        return pltpu.make_async_remote_copy(
            src_ref=part.at[s, pl.ds(t * rows, rows)],
            dst_ref=inbox.at[s, me],
            send_sem=rs_send.at[s, t],
            recv_sem=rs_recv.at[s, me],
            device_id={"slab": t * stride},
            device_id_type=MESH,
        )

    def rs_start(s):
        @pl.loop(0, owners)
        def _(t):
            @pl.when(t * stride != me)
            def _():
                rs_copy(s, t).start()

    mine = me // stride

    def ag_copy(s, d):
        return pltpu.make_async_remote_copy(
            src_ref=share.at[s],
            dst_ref=full.at[s, pl.ds(mine * rows, rows)],
            send_sem=ag_send.at[s, d],
            recv_sem=ag_recv.at[s, mine],
            device_id={"slab": lax.rem(me + d, n)},
            device_id_type=MESH,
        )

    def owner(f):
        if stride == 1:
            f()
        else:
            pl.when(me == mine * stride)(f)

    def rs_finish(s):
        @pl.loop(0, owners)
        def _(t):
            @pl.when(t * stride != me)
            def _():
                rs_copy(s, t).wait_send()

        @owner
        def _():
            share[s] = part[s, pl.ds(mine * rows, rows)]

            @pl.loop(1, n)
            def _(d):
                src = lax.rem(me + d, n)
                pltpu.make_async_remote_copy(
                    src_ref=inbox.at[s, src],
                    dst_ref=inbox.at[s, src],
                    send_sem=rs_send.at[s, 0],
                    recv_sem=rs_recv.at[s, src],
                    device_id={"slab": src},
                    device_id_type=MESH,
                ).wait_recv()
                share[s] = share[s] + inbox[s, src]

            @pl.loop(1, n)
            def _(d):
                ag_copy(s, d).start()

            full[s, pl.ds(mine * rows, rows)] = share[s]

    def ag_finish(s):
        @owner
        def _():
            @pl.loop(1, n)
            def _(d):
                ag_copy(s, d).wait_send()

        @pl.loop(0, owners)
        def _(t):
            @pl.when(t * stride != me)
            def _():
                pltpu.make_async_remote_copy(
                    src_ref=share.at[s],
                    dst_ref=full.at[s, pl.ds(t * rows, rows)],
                    send_sem=ag_send.at[s, 0],
                    recv_sem=ag_recv.at[s, t],
                    device_id={"slab": t * stride},
                    device_id_type=MESH,
                ).wait_recv()

    batch = max(d for d in range(1, 9) if cells % (2 * d) == 0)
    gacc[...] = jnp.zeros_like(gacc)

    @pl.loop(0, cells, step=batch)
    def _(c):
        lhs = jnp.concatenate([wt[c + i] for i in range(batch)], axis=1)
        gacc[...] += jnp.dot(
            lhs, twice(wa, c + 2, batch), preferred_element_type=F32
        )

    part[0] = fold(gacc)
    rs_start(0)

    gacc[...] = jnp.zeros_like(gacc)

    def half_image(c):
        lhs = jnp.concatenate(
            [half_t[on_idx[c]], hop_t[hop_idx[2, c]], hop_t[hop_idx[3, c]]], axis=1
        )
        return fold(jnp.dot(lhs, twice(wa, c + 2, 3), preferred_element_type=F32))

    def project(c):
        images = []
        for i in range(batch):
            hi, lo = split2(half_image(c + i))
            both = jnp.concatenate([hi, lo], axis=1)
            images += [both, both]
        lhs = jnp.concatenate([wt[c + i] for i in range(batch)], axis=1)
        gacc[...] += jnp.dot(
            lhs, jnp.concatenate(images, axis=0), preferred_element_type=F32
        )

    middle = cells // 2

    @pl.loop(0, middle, step=batch)
    def _(c):
        project(c)

    rs_finish(0)
    halo_wait(4, fb, wa)

    @pl.loop(middle, cells, step=batch)
    def _(c):
        project(c)

    part[1] = fold(gacc)
    rs_start(1)

    ag_finish(0)
    aug[:, 0:width] = full[0]
    row = lax.broadcasted_iota(jnp.int32, (width, width), 0)
    col = lax.broadcasted_iota(jnp.int32, (width, width), 1)
    aug[:, width : 2 * width] = jnp.where(row == col, 1.0, 0.0).astype(F32)

    def chol_block(b):
        base = 8 * b
        panel = aug[base : base + 8, :]
        s = {}
        for i in range(8):
            for k in range(i, 8):
                s[i, k] = jnp.broadcast_to(
                    panel[i : i + 1, base + k : base + k + 1], (1, 2 * width)
                )
        lines = [panel[i : i + 1, :] for i in range(8)]
        done = []
        for i in range(8):
            inv = lax.rsqrt(s[i, i])
            line = lines[i] * inv
            done.append(line)
            low = {k: s[i, k] * inv for k in range(i + 1, 8)}
            for k in range(i + 1, 8):
                lines[k] = lines[k] - low[k] * line
                for m in range(k, 8):
                    s[k, m] = s[k, m] - low[k] * low[m]
        upper = jnp.concatenate(done, axis=0)
        aug[base : base + 8, :] = upper
        if base + 8 < width:
            hi, mid, lo = split3(upper)
            left = jnp.concatenate([hi, hi, mid, hi, mid, lo], axis=0)[:, 0:width]
            right = jnp.concatenate([hi, mid, hi, lo, mid, hi], axis=0)
            update = lax.dot_general(
                left.T.astype(BF),
                right.astype(BF),
                (((1,), (0,)), ((), ())),
                preferred_element_type=F32,
            )
            aug[base + 8 :, :] = aug[base + 8 :, :] - update[base + 8 :, :]

    blocks = width // 8
    early = 3 * blocks // 8
    for b in range(early):
        chol_block(b)
    rs_finish(1)
    for b in range(early, blocks):
        chol_block(b)
    ag_finish(1)

    inv_out[...] = aug[:, width : 2 * width]
    upper = full[1]
    proj_out[...] = upper + upper.T
    store.wait()


def finish(factor, wide, inv, proj, basis, reduced, weights):
    count, orb, double = wide.shape
    width = double // 2
    inverse = inv[...]

    @pl.when(pl.program_id(0) == 0)
    def _():
        hi, lo = split2(inverse.T * factor)
        for i in range(2):
            weights[i * width : (i + 1) * width, 0:width] = hi
            weights[i * width : (i + 1) * width, width : 2 * width] = lo

    both = jnp.dot(
        wide[...].reshape(count * orb, double),
        weights[...],
        preferred_element_type=F32,
    )
    basis[...] = (both[:, :width] + both[:, width:]).reshape(count, orb, width)

    @pl.when(pl.program_id(0) == jnp.minimum(1, pl.num_programs(0) - 1))
    def _():
        right = dot_halves(inverse, proj[...])
        reduced[...] = dot_halves(right, inverse.T)


def local(states, onsite_blocks, hop_blocks, onsite_index, hop_index):
    cells, orb, width = states.shape
    n = lax.axis_size("slab")
    owners = min(n, width // 8)
    rows = width // owners
    non, nhop = onsite_blocks.shape[0], hop_blocks.shape[0]
    vmem = pl.BlockSpec(memory_space=pltpu.VMEM)
    hbm = pl.BlockSpec(memory_space=pl.ANY)
    smem = pl.BlockSpec(memory_space=pltpu.SMEM)
    field = pltpu.VMEM((cells, orb, width), F32)
    wide = pltpu.VMEM((cells + 4, orb, 2 * width), BF)
    halo = pltpu.VMEM((DEGREE + 1, 2, orb, width), F32)
    dma = pltpu.SemaphoreType.DMA
    current, inverse, projected = pl.pallas_call(
        functools.partial(kernel, n, owners),
        out_shape=(
            jax.ShapeDtypeStruct((cells, orb, 2 * width), BF),
            jax.ShapeDtypeStruct((width, width), F32),
            jax.ShapeDtypeStruct((width, width), F32),
        ),
        in_specs=[smem, smem, hbm, hbm, hbm],
        out_specs=(hbm, vmem, vmem),
        scratch_shapes=[
            field,
            pltpu.VMEM((non, orb, orb), F32),
            pltpu.VMEM((nhop, orb, orb), F32),
            pltpu.VMEM((non, orb, 2 * orb), BF),
            pltpu.VMEM((non, orb, 2 * orb), BF),
            pltpu.VMEM((nhop, orb, 2 * orb), BF),
            pltpu.VMEM((nhop, orb, 2 * orb), BF),
            wide,
            wide,
            field,
            field,
            pltpu.VMEM((cells, width, 2 * orb), BF),
            halo,
            halo,
            pltpu.VMEM((width, 2 * width), F32),
            pltpu.VMEM((2, width, width), F32),
            pltpu.VMEM((2, n, rows, width), F32),
            pltpu.VMEM((2, rows, width), F32),
            pltpu.VMEM((2, width, width), F32),
            pltpu.VMEM((width, 2 * width), F32),
            dma((DEGREE + 1, 2)),
            dma((DEGREE + 1, 2)),
            dma((2, owners)),
            dma((2, n)),
            dma((2, n)),
            dma((2, owners)),
            dma((3,)),
            dma,
        ],
        compiler_params=pltpu.CompilerParams(
            collective_id=0, has_side_effects=True, vmem_limit_bytes=60 * 2**20
        ),
        name="filter",
    )(hop_index.T, onsite_index, states, onsite_blocks, hop_blocks)
    total = cells * n
    factor = float(total * orb) ** 0.5
    count = max(d for d in range(1, 17) if cells % d == 0)
    square = pl.BlockSpec((width, width), lambda i: (0, 0))
    basis, reduced = pl.pallas_call(
        functools.partial(finish, factor),
        grid=(cells // count,),
        out_shape=(
            jax.ShapeDtypeStruct((cells, orb, width), F32),
            jax.ShapeDtypeStruct((width, width), F32),
        ),
        in_specs=[
            pl.BlockSpec((count, orb, 2 * width), lambda i: (i, 0, 0)),
            square,
            square,
        ],
        out_specs=(pl.BlockSpec((count, orb, width), lambda i: (i, 0, 0)), square),
        scratch_shapes=[pltpu.VMEM((2 * width, 2 * width), BF)],
        compiler_params=pltpu.CompilerParams(vmem_limit_bytes=60 * 2**20),
        name="finish",
    )(current, inverse, projected)
    return (basis, reduced)


def solution(mesh):
    placed = (
        P(("grp", "slab"), None, None),
        P(),
        P(),
        P(("grp", "slab")),
        P(("grp", "slab"), None),
    )
    return jax.shard_map(
        local,
        mesh=mesh,
        in_specs=placed,
        out_specs=(P(("grp", "slab"), None, None), P("grp", None)),
        check_vma=False,
    )
```

```python
import functools

import jax
import jax.numpy as jnp
from jax import lax
from jax.experimental import pallas as pl
from jax.experimental.pallas import tpu as pltpu
from jax.sharding import PartitionSpec as P

DEGREE = 4
MESH = pl.DeviceIdType.MESH
BF = jnp.bfloat16
F32 = jnp.float32


def split2(x):
    hi = x.astype(BF)
    lo = (x - hi.astype(F32)).astype(BF)
    return hi, lo


def dot_halves(a, b):
    b_both = jnp.concatenate(split2(b), axis=1)
    both = jnp.dot(
        jnp.concatenate(split2(a), axis=1),
        jnp.concatenate([b_both, b_both], axis=0),
        preferred_element_type=F32,
    )
    half = b.shape[1]
    return both[:, :half] + both[:, half:]


def split3(x):
    hi = x.astype(BF).astype(F32)
    rest = x - hi
    mid = rest.astype(BF).astype(F32)
    return hi, mid, rest - mid


def kernel(
    n,
    owners,
    hop_idx,
    on_idx,
    states_hbm,
    onsite_hbm,
    hop_hbm,
    wide_out,
    inv_out,
    proj_out,
    states,
    onsite,
    hop,
    sym_t,
    half_t,
    hop_t,
    hopt_t,
    wa,
    wb,
    fa,
    fb,
    wt,
    halo_l,
    halo_r,
    gacc,
    part,
    inbox,
    share,
    full,
    aug,
    halo_send,
    halo_recv,
    rs_send,
    rs_recv,
    ag_send,
    ag_recv,
    load_sem,
    store_sem,
):
    me = lax.axis_index("slab")
    cells, orb, width = states.shape
    stride = n // owners
    rows = width // owners
    non = onsite.shape[0]
    nhop = hop.shape[0]

    barrier = pltpu.get_barrier_semaphore()

    @pl.loop(1, n)
    def _(d):
        pl.semaphore_signal(
            barrier, inc=1, device_id={"slab": lax.rem(me + d, n)}, device_id_type=MESH
        )

    loads = [
        pltpu.make_async_copy(src, dst, load_sem.at[i])
        for i, (src, dst) in enumerate(
            ((hop_hbm, hop), (onsite_hbm, onsite), (states_hbm, states))
        )
    ]
    for load in loads:
        load.start()

    def put(w, at, x):
        hi, lo = split2(x)
        w[at, :, 0:width] = hi
        w[at, :, width : 2 * width] = lo

    def table(ref, at, x):
        hi, lo = split2(x)
        ref[at, :, 0:orb] = hi
        ref[at, :, orb : 2 * orb] = lo

    zero2 = jnp.zeros((2, orb, 2 * width), BF)
    for w in (wa, wb):
        w[0:2] = zero2
        w[cells + 2 : cells + 4] = zero2

    pl.semaphore_wait(barrier, n - 1)

    def halo(k, src):
        left = pltpu.make_async_remote_copy(
            src_ref=src.at[0:2],
            dst_ref=halo_r.at[k],
            send_sem=halo_send.at[k, 0],
            recv_sem=halo_recv.at[k, 0],
            device_id={"slab": jnp.maximum(me - 1, 0)},
            device_id_type=MESH,
        )
        right = pltpu.make_async_remote_copy(
            src_ref=src.at[cells - 2 : cells],
            dst_ref=halo_l.at[k],
            send_sem=halo_send.at[k, 1],
            recv_sem=halo_recv.at[k, 1],
            device_id={"slab": jnp.minimum(me + 1, n - 1)},
            device_id_type=MESH,
        )
        return left, right

    def halo_start(k, src):
        left, right = halo(k, src)
        pl.when(me > 0)(left.start)
        if k < DEGREE:
            pl.when(me < n - 1)(right.start)

    def halo_wait(k, src, w):
        left, right = halo(k, src)

        @pl.when(me > 0)
        def _():
            left.wait_send()
            if k < DEGREE:
                right.wait_recv()
                for i in range(2):
                    put(w, i, halo_l[k, i])

        @pl.when(me < n - 1)
        def _():
            if k < DEGREE:
                right.wait_send()
            left.wait_recv()
            for i in range(2):
                put(w, cells + 2 + i, halo_r[k, i])

    halo_start(0, states_hbm)

    loads[0].wait()
    loads[1].wait()

    @pl.loop(0, non, unroll=True)
    def _(i):
        block = onsite[i]
        sym = 0.5 * (block + block.T)
        table(sym_t, i, sym)
        table(half_t, i, 0.5 * sym)

    @pl.loop(0, nhop, unroll=4)
    def _(i):
        block = hop[i]
        table(hop_t, i, block)
        table(hopt_t, i, block.T)

    loads[2].wait()

    @pl.loop(0, cells, unroll=4)
    def _(c):
        put(wa, c + 2, states[c])

    halo_wait(0, states_hbm, wa)

    def fold(acc):
        return acc[:, :width] + acc[:, width:]

    def twice(w, at, count):
        parts = []
        for i in range(count):
            block = w[at + i]
            parts += [block, block]
        return jnp.concatenate(parts, axis=0)

    def apply_cell(w, c):
        lhs = jnp.concatenate(
            [
                hopt_t[hop_idx[0, c]],
                hopt_t[hop_idx[1, c]],
                sym_t[on_idx[c]],
                hop_t[hop_idx[2, c]],
                hop_t[hop_idx[3, c]],
            ],
            axis=1,
        )
        return fold(jnp.dot(lhs, twice(w, c, 5), preferred_element_type=F32))

    def step(k, w, w_next, cur, prev, out):
        def one(c):
            image = apply_cell(w, c)
            if k == 0:
                new = (image - 1.5 * cur[c]) * (1.0 / 3.0)
            else:
                new = (image - 1.5 * cur[c]) * (2.0 / 3.0) - prev[c]
            out[c] = new
            put(w_next, c + 2, new)
            if k == DEGREE - 1:
                hi, lo = split2(new.T)
                wt[c, :, 0:orb] = hi
                wt[c, :, orb : 2 * orb] = lo

        for c in (0, 1, cells - 2, cells - 1):
            one(c)
        halo_start(k + 1, out)

        inner = cells - 4
        group = max(d for d in range(1, 29) if inner % d == 0)

        @pl.loop(2, cells - 2, step=group)
        def _(c):
            for i in range(group):
                one(c + i)

    step(0, wa, wb, states, None, fa)
    halo_wait(1, fa, wb)
    step(1, wb, wa, fa, states, fb)
    halo_wait(2, fb, wa)
    step(2, wa, wb, fb, fa, fa)
    halo_wait(3, fa, wb)
    step(3, wb, wa, fa, fb, fb)
    store = pltpu.make_async_copy(
        wa.at[2 : cells + 2], wide_out, store_sem
    )
    store.start()

    def rs_copy(s, t):
        return pltpu.make_async_remote_copy(
            src_ref=part.at[s, pl.ds(t * rows, rows)],
            dst_ref=inbox.at[s, me],
            send_sem=rs_send.at[s, t],
            recv_sem=rs_recv.at[s, me],
            device_id={"slab": t * stride},
            device_id_type=MESH,
        )

    def rs_start(s):
        @pl.loop(0, owners)
        def _(t):
            @pl.when(t * stride != me)
            def _():
                rs_copy(s, t).start()

    mine = me // stride

    def ag_copy(s, d):
        return pltpu.make_async_remote_copy(
            src_ref=share.at[s],
            dst_ref=full.at[s, pl.ds(mine * rows, rows)],
            send_sem=ag_send.at[s, d],
            recv_sem=ag_recv.at[s, mine],
            device_id={"slab": lax.rem(me + d, n)},
            device_id_type=MESH,
        )

    def owner(f):
        if stride == 1:
            f()
        else:
            pl.when(me == mine * stride)(f)

    def rs_finish(s):
        @pl.loop(0, owners)
        def _(t):
            @pl.when(t * stride != me)
            def _():
                rs_copy(s, t).wait_send()

        @owner
        def _():
            share[s] = part[s, pl.ds(mine * rows, rows)]

            @pl.loop(1, n)
            def _(d):
                src = lax.rem(me + d, n)
                pltpu.make_async_remote_copy(
                    src_ref=inbox.at[s, src],
                    dst_ref=inbox.at[s, src],
                    send_sem=rs_send.at[s, 0],
                    recv_sem=rs_recv.at[s, src],
                    device_id={"slab": src},
                    device_id_type=MESH,
                ).wait_recv()
                share[s] = share[s] + inbox[s, src]

            @pl.loop(1, n)
            def _(d):
                ag_copy(s, d).start()

            full[s, pl.ds(mine * rows, rows)] = share[s]

    def ag_finish(s):
        @owner
        def _():
            @pl.loop(1, n)
            def _(d):
                ag_copy(s, d).wait_send()

        @pl.loop(0, owners)
        def _(t):
            @pl.when(t * stride != me)
            def _():
                pltpu.make_async_remote_copy(
                    src_ref=share.at[s],
                    dst_ref=full.at[s, pl.ds(t * rows, rows)],
                    send_sem=ag_send.at[s, 0],
                    recv_sem=ag_recv.at[s, t],
                    device_id={"slab": t * stride},
                    device_id_type=MESH,
                ).wait_recv()

    batch = max(d for d in range(1, 17) if cells % (2 * d) == 0)
    gacc[...] = jnp.zeros_like(gacc)

    @pl.loop(0, cells, step=batch)
    def _(c):
        lhs = jnp.concatenate([wt[c + i] for i in range(batch)], axis=1)
        gacc[...] += jnp.dot(
            lhs, twice(wa, c + 2, batch), preferred_element_type=F32
        )

    part[0] = fold(gacc)
    rs_start(0)

    gacc[...] = jnp.zeros_like(gacc)

    def half_image(c):
        lhs = jnp.concatenate(
            [half_t[on_idx[c]], hop_t[hop_idx[2, c]], hop_t[hop_idx[3, c]]], axis=1
        )
        return fold(jnp.dot(lhs, twice(wa, c + 2, 3), preferred_element_type=F32))

    def project(c):
        images = []
        for i in range(batch):
            hi, lo = split2(half_image(c + i))
            both = jnp.concatenate([hi, lo], axis=1)
            images += [both, both]
        lhs = jnp.concatenate([wt[c + i] for i in range(batch)], axis=1)
        gacc[...] += jnp.dot(
            lhs, jnp.concatenate(images, axis=0), preferred_element_type=F32
        )

    middle = cells // 2

    @pl.loop(0, middle, step=batch)
    def _(c):
        project(c)

    rs_finish(0)
    halo_wait(4, fb, wa)

    @pl.loop(middle, cells, step=batch)
    def _(c):
        project(c)

    part[1] = fold(gacc)
    rs_start(1)

    ag_finish(0)
    aug[:, 0:width] = full[0]
    row = lax.broadcasted_iota(jnp.int32, (width, width), 0)
    col = lax.broadcasted_iota(jnp.int32, (width, width), 1)
    aug[:, width : 2 * width] = jnp.where(row == col, 1.0, 0.0).astype(F32)

    def chol_block(b):
        base = 8 * b
        panel = aug[base : base + 8, :]
        s = {}
        for i in range(8):
            for k in range(i, 8):
                s[i, k] = jnp.broadcast_to(
                    panel[i : i + 1, base + k : base + k + 1], (1, 2 * width)
                )
        lines = [panel[i : i + 1, :] for i in range(8)]
        done = []
        for i in range(8):
            inv = lax.rsqrt(s[i, i])
            line = lines[i] * inv
            done.append(line)
            low = {k: s[i, k] * inv for k in range(i + 1, 8)}
            for k in range(i + 1, 8):
                lines[k] = lines[k] - low[k] * line
                for m in range(k, 8):
                    s[k, m] = s[k, m] - low[k] * low[m]
        upper = jnp.concatenate(done, axis=0)
        aug[base : base + 8, :] = upper
        if base + 8 < width:
            hi, mid, lo = split3(upper)
            left = jnp.concatenate([hi, hi, mid, hi, mid, lo], axis=0)[:, 0:width]
            right = jnp.concatenate([hi, mid, hi, lo, mid, hi], axis=0)
            update = lax.dot_general(
                left.T.astype(BF),
                right.astype(BF),
                (((1,), (0,)), ((), ())),
                preferred_element_type=F32,
            )
            aug[base + 8 :, :] = aug[base + 8 :, :] - update[base + 8 :, :]

    blocks = width // 8
    early = 3 * blocks // 8
    for b in range(early):
        chol_block(b)
    rs_finish(1)
    for b in range(early, blocks):
        chol_block(b)
    ag_finish(1)

    inv_out[...] = aug[:, width : 2 * width]
    upper = full[1]
    proj_out[...] = upper + upper.T
    store.wait()


def finish(factor, wide, inv, proj, basis, reduced, weights):
    count, orb, double = wide.shape
    width = double // 2
    inverse = inv[...]

    @pl.when(pl.program_id(0) == 0)
    def _():
        hi, lo = split2(inverse.T * factor)
        for i in range(2):
            weights[i * width : (i + 1) * width, 0:width] = hi
            weights[i * width : (i + 1) * width, width : 2 * width] = lo

    both = jnp.dot(
        wide[...].reshape(count * orb, double),
        weights[...],
        preferred_element_type=F32,
    )
    basis[...] = (both[:, :width] + both[:, width:]).reshape(count, orb, width)

    @pl.when(pl.program_id(0) == jnp.minimum(1, pl.num_programs(0) - 1))
    def _():
        right = dot_halves(inverse, proj[...])
        reduced[...] = dot_halves(right, inverse.T)


def local(states, onsite_blocks, hop_blocks, onsite_index, hop_index):
    cells, orb, width = states.shape
    n = lax.axis_size("slab")
    owners = min(n, width // 8)
    rows = width // owners
    non, nhop = onsite_blocks.shape[0], hop_blocks.shape[0]
    vmem = pl.BlockSpec(memory_space=pltpu.VMEM)
    hbm = pl.BlockSpec(memory_space=pl.ANY)
    smem = pl.BlockSpec(memory_space=pltpu.SMEM)
    field = pltpu.VMEM((cells, orb, width), F32)
    wide = pltpu.VMEM((cells + 4, orb, 2 * width), BF)
    halo = pltpu.VMEM((DEGREE + 1, 2, orb, width), F32)
    dma = pltpu.SemaphoreType.DMA
    current, inverse, projected = pl.pallas_call(
        functools.partial(kernel, n, owners),
        out_shape=(
            jax.ShapeDtypeStruct((cells, orb, 2 * width), BF),
            jax.ShapeDtypeStruct((width, width), F32),
            jax.ShapeDtypeStruct((width, width), F32),
        ),
        in_specs=[smem, smem, hbm, hbm, hbm],
        out_specs=(hbm, vmem, vmem),
        scratch_shapes=[
            field,
            pltpu.VMEM((non, orb, orb), F32),
            pltpu.VMEM((nhop, orb, orb), F32),
            pltpu.VMEM((non, orb, 2 * orb), BF),
            pltpu.VMEM((non, orb, 2 * orb), BF),
            pltpu.VMEM((nhop, orb, 2 * orb), BF),
            pltpu.VMEM((nhop, orb, 2 * orb), BF),
            wide,
            wide,
            field,
            field,
            pltpu.VMEM((cells, width, 2 * orb), BF),
            halo,
            halo,
            pltpu.VMEM((width, 2 * width), F32),
            pltpu.VMEM((2, width, width), F32),
            pltpu.VMEM((2, n, rows, width), F32),
            pltpu.VMEM((2, rows, width), F32),
            pltpu.VMEM((2, width, width), F32),
            pltpu.VMEM((width, 2 * width), F32),
            dma((DEGREE + 1, 2)),
            dma((DEGREE + 1, 2)),
            dma((2, owners)),
            dma((2, n)),
            dma((2, n)),
            dma((2, owners)),
            dma((3,)),
            dma,
        ],
        compiler_params=pltpu.CompilerParams(
            collective_id=0, has_side_effects=True, vmem_limit_bytes=60 * 2**20
        ),
        name="filter",
    )(hop_index.T, onsite_index, states, onsite_blocks, hop_blocks)
    total = cells * n
    factor = float(total * orb) ** 0.5
    count = max(d for d in range(1, 17) if cells % d == 0)
    square = pl.BlockSpec((width, width), lambda i: (0, 0))
    basis, reduced = pl.pallas_call(
        functools.partial(finish, factor),
        grid=(cells // count,),
        out_shape=(
            jax.ShapeDtypeStruct((cells, orb, width), F32),
            jax.ShapeDtypeStruct((width, width), F32),
        ),
        in_specs=[
            pl.BlockSpec((count, orb, 2 * width), lambda i: (i, 0, 0)),
            square,
            square,
        ],
        out_specs=(pl.BlockSpec((count, orb, width), lambda i: (i, 0, 0)), square),
        scratch_shapes=[pltpu.VMEM((2 * width, 2 * width), BF)],
        compiler_params=pltpu.CompilerParams(vmem_limit_bytes=60 * 2**20),
        name="finish",
    )(current, inverse, projected)
    return (basis, reduced)


def solution(mesh):
    placed = (
        P(("grp", "slab"), None, None),
        P(),
        P(),
        P(("grp", "slab")),
        P(("grp", "slab"), None),
    )
    return jax.shard_map(
        local,
        mesh=mesh,
        in_specs=placed,
        out_specs=(P(("grp", "slab"), None, None), P("grp", None)),
        check_vma=False,
    )
```
